32 devices in a mesh: dp: 8 (over z, x), fly: 4 (over y, core).
Axes of the slice: x: 2, y: 2, z: 4, core: 2. Of those that a mesh axis runs over, the one named last changes fastest.
Arguments:
- tokens: bfloat16 [1024, 8192], P('dp', 'fly'), may hold values from -6 to 6
- hidden_grad: bfloat16 [1024, 16384], P('dp', 'fly'), may hold values from -6 to 6
- w_up: bfloat16 [6, 256, 16384], P(None, 'dp', 'fly'), may hold values from -0.15625 to 0.15625
- pattern: int32 [6, 64], P(None, 'fly'), may hold values 0 or 1
Outputs:
- input_grad: bfloat16 [1024, 8192], P('dp', 'fly')
- weight_grad: float32 [6, 256, 16384], P(None, 'dp', 'fly')
The draws below stay inside these ranges and needn't reach their ends.
Inputs may be any that keep to these rules, and one draw needn't show every extreme that they name: pattern[t, f] is 1 where block f of factor t is kept and 0 where it is dropped.
All inputs are finite; a program needn't handle non-finite values.
Results may differ from the reference program's by a relative error of at most 0.0049.
Values may be sent and summed in bfloat16 or wider, within the bound.
A program may use at most 128 MiB of HBM per device.

```python
import jax
import jax.numpy as jnp
from jax import lax

BS = 256
SECTIONS = 6
D = 8192
FF = 16384
TOK_DEV = 128
REPLICAS = 8
TOKENS = 1024


def set_ends(drawn, stream_key, low, largest):
    place = [jax.random.randint(jax.random.fold_in(stream_key, axis), (), 0, length) for axis, length in enumerate(drawn.shape)]
    main_axis = drawn.shape.index(max(drawn.shape))
    beside = place[:main_axis] + [(place[main_axis] + 1) % drawn.shape[main_axis]] + place[main_axis + 1:]
    return drawn.at[tuple(place)].set(low).at[tuple(beside)].set(largest)


def block_scale(key, shape, cuts, low, largest):
    def one(axis_at, blocks):
        heights = jax.random.uniform(jax.random.fold_in(jax.random.fold_in(key, 6), axis_at), (blocks,), jnp.float32, low / len(cuts), largest / len(cuts))
        return jnp.repeat(jnp.exp(heights), shape[axis_at] // blocks).reshape((-1,) + (1,) * (len(shape) - axis_at - 1))

    level = one(*cuts[0])
    for cut in cuts[1:]:
        level = level * one(*cut)
    return level


def gaussian(own_key, shape, spread, most, shards=(), dtype=jnp.bfloat16):
    level = block_scale(own_key, shape, shards, -0.22, 0.18) if shards else 1.0
    array = jax.random.normal(own_key, shape, jnp.float32) * spread * level
    return jnp.minimum(jnp.maximum(array, -most), most).astype(dtype)


def setup_inputs(seed: int = 0) -> dict:
    splits = jax.random.split(jax.random.key(seed), 5)
    return {
        "tokens": gaussian(splits[0], (TOKENS, D), 1.0, 6.0, ((0, 8), (1, 4))),
        "hidden_grad": gaussian(splits[1], (TOKENS, FF), 1.0, 6.0, ((0, 8), (1, 4))),
        "w_up": gaussian(splits[2], (SECTIONS, BS, FF), (SECTIONS * BS) ** -0.5, 0.15625, ((1, 8), (2, 4))),
        "pattern": set_ends((jax.random.randint(splits[3], (SECTIONS, FF // BS), 0, 4) < 3).astype(jnp.int32), jax.random.fold_in(splits[3], 1), 0, 1),
    }


def flip_blocks(values, stride):
    if stride == 0:
        return values
    row_count, block_count, inner_size = values.shape
    shaped = values.reshape(row_count, block_count // (2 * stride), 2, stride, inner_size)
    return shaped[:, :, ::-1].reshape(row_count, block_count, inner_size)


def stride_of(factor):
    return 0 if factor == 0 else 2 ** (factor - 1)


def reference(tokens, hidden_grad, w_up, pattern):
    block_count = D // BS
    group_width = FF // block_count
    keep_cols = jnp.broadcast_to(pattern[:, :, None], (SECTIONS, FF // BS, BS)).reshape(SECTIONS, FF)
    masked = w_up * keep_cols.astype(jnp.bfloat16)[:, None, :]
    masked_f = masked.astype(jnp.float32).reshape(SECTIONS, BS, block_count, group_width)
    keep_f = keep_cols.astype(jnp.float32)
    token_sets = tokens.reshape(REPLICAS, TOK_DEV, D)
    grad_sets = hidden_grad.reshape(REPLICAS, TOK_DEV, FF)

    def replica_step(running, inputs_pair):
        token_rows, grad_rows = inputs_pair
        token_blocks = token_rows.astype(jnp.float32).reshape(TOK_DEV, block_count, BS)
        gathered = [flip_blocks(token_blocks, stride_of(factor)) for factor in range(SECTIONS)]
        pre_act = jnp.zeros((TOK_DEV, block_count, group_width), jnp.float32)
        for factor in range(SECTIONS):
            pre_act = pre_act + jnp.einsum("ngb,bgc->ngc", gathered[factor], masked_f[factor])
        squash = jax.nn.sigmoid(pre_act)
        derivative = squash * (1.0 + pre_act * (1.0 - squash))
        grad_pre = (grad_rows.astype(jnp.float32).reshape(TOK_DEV, block_count, group_width) * derivative).astype(jnp.bfloat16)
        grad_pre_f = grad_pre.astype(jnp.float32)
        input_total = jnp.zeros((TOK_DEV, block_count, BS), jnp.float32)
        updated = []
        for factor in range(SECTIONS):
            contrib = jnp.einsum("ngc,bgc->ngb", grad_pre_f, masked_f[factor])
            input_total = input_total + flip_blocks(contrib, stride_of(factor))
            product_term = jnp.einsum("ngb,ngc->bgc", gathered[factor], grad_pre_f).reshape(BS, FF)
            product_term = product_term * keep_f[factor][None, :]
            updated.append(running[factor] + product_term)
        return jnp.stack(updated), input_total.reshape(TOK_DEV, D).astype(jnp.bfloat16)

    initial = jnp.zeros((SECTIONS, BS, FF), jnp.float32)
    grad_total, input_rows = lax.scan(replica_step, initial, (token_sets, grad_sets))
    weight_grad = grad_total * (1.0 / REPLICAS)
    return input_rows.reshape(TOKENS, D), weight_grad
```

```python
import jax
import jax.numpy as jnp
from jax import lax
from jax.sharding import PartitionSpec as P

BS = 256


def partner_2(block, axis, bit):
    count = lax.axis_size(axis)
    route = []
    for low in range(count):
        high = low | 1 << bit
        if high != low and high < count:
            route += [(low, high), (high, low)]
    return lax.ppermute(block, axis, route)


def shifted(value, axis, by):
    devices = lax.axis_size(axis)
    return lax.ppermute(value, axis, [(i, (i + by) % devices) for i in range(devices)])


def flip_blocks(values, stride):
    if stride == 0:
        return values
    row_count, block_count, inner_size = values.shape
    shaped = values.reshape(row_count, block_count // (2 * stride), 2, stride, inner_size)
    return shaped[:, :, ::-1].reshape(row_count, block_count, inner_size)


def stride_of(factor):
    return 0 if factor == 0 else 2 ** (factor - 1)


def pick_rows(stacked, index, replicas):
    return lax.dynamic_index_in_dim(stacked, index % replicas, 1, keepdims=False)


def body_general(tokens, hidden_grad, w_up, pattern):
    row_count, local_width = tokens.shape
    factor_count = w_up.shape[0]
    hidden_width = hidden_grad.shape[1]
    local_blocks = local_width // BS
    group_width = hidden_width // local_blocks
    weights = lax.all_gather(w_up, "dp", axis=1, tiled=True)
    keep_cols = jnp.broadcast_to(pattern[:, :, None], (factor_count, pattern.shape[1], BS)).reshape(
        factor_count, hidden_width
    )
    masked = (weights * keep_cols.astype(jnp.bfloat16)[:, None, :]).reshape(
        factor_count, BS, local_blocks, group_width
    )
    keep_f = keep_cols.astype(jnp.float32)
    token_blocks = tokens.reshape(row_count, local_blocks, BS)
    gathered = []
    for factor in range(factor_count):
        stride = stride_of(factor)
        if stride < local_blocks:
            gathered.append(flip_blocks(token_blocks, stride))
        else:
            bit_number = (stride // local_blocks).bit_length() - 1
            partner = partner_2(tokens, "fly", bit_number)
            gathered.append(partner.reshape(row_count, local_blocks, BS))
    pre_act = jnp.zeros((row_count, local_blocks, group_width), jnp.float32)
    for factor in range(factor_count):
        pre_act = pre_act + jnp.einsum(
            "ngb,bgc->ngc", gathered[factor], masked[factor], preferred_element_type=jnp.float32
        )
    squash = jax.nn.sigmoid(pre_act)
    derivative = squash * (1.0 + pre_act * (1.0 - squash))
    grad_pre = (
        hidden_grad.reshape(row_count, local_blocks, group_width).astype(jnp.float32) * derivative
    ).astype(jnp.bfloat16)
    input_total = jnp.zeros((row_count, local_blocks, BS), jnp.float32)
    for factor in range(factor_count):
        stride = stride_of(factor)
        contrib = jnp.einsum(
            "ngc,bgc->ngb", grad_pre, masked[factor], preferred_element_type=jnp.float32
        )
        if stride < local_blocks:
            input_total = input_total + flip_blocks(contrib, stride)
        else:
            bit_number = (stride // local_blocks).bit_length() - 1
            returned = partner_2(contrib.reshape(row_count, local_width), "fly", bit_number)
            input_total = input_total + returned.reshape(row_count, local_blocks, BS)
    input_grad = input_total.reshape(row_count, local_width).astype(jnp.bfloat16)
    replicas = lax.axis_size("dp")
    place = lax.axis_index("dp")
    row_share = BS // replicas
    terms = []
    for factor in range(factor_count):
        product_term = jnp.einsum(
            "ngb,ngc->bgc", gathered[factor], grad_pre, preferred_element_type=jnp.float32
        )
        terms.append(product_term.reshape(BS, hidden_width) * keep_f[factor][None, :])
    term_stack = jnp.stack(terms).reshape(factor_count, replicas, row_share, hidden_width)

    def turn_one(step, carry):
        return shifted(carry, "dp", 1) + pick_rows(
            term_stack, place - step - 2 + 2 * replicas, replicas
        )

    summed = lax.fori_loop(
        0, replicas - 1, turn_one, pick_rows(term_stack, place - 1 + replicas, replicas)
    )
    weight_grad = summed * (1.0 / replicas)
    return (input_grad, weight_grad)


def exchanged(value, factor, groups):
    stride = stride_of(factor)
    if stride == 0:
        return value
    axis, by = ("dp", stride) if stride < groups else ("fly", stride // groups)
    return lax.ppermute(value, axis, [(i, i ^ by) for i in range(lax.axis_size(axis))])


def body_by_group(tokens, hidden_grad, w_up, pattern):
    groups = lax.axis_size("dp")
    place = lax.axis_index("dp")
    factor_count = w_up.shape[0]
    group_width = hidden_grad.shape[1] // groups
    own = lax.all_to_all(tokens, "dp", 1, 0, tiled=True)
    weights = lax.all_to_all(w_up, "dp", 2, 1, tiled=True)
    upstream = lax.all_to_all(hidden_grad, "dp", 1, 0, tiled=True)
    per_group = group_width // BS
    keep = lax.dynamic_slice_in_dim(pattern, place * per_group, per_group, 1)
    keep_cols = jnp.broadcast_to(keep[:, :, None], keep.shape + (BS,)).reshape(factor_count, 1, group_width)
    masked = (weights * keep_cols.astype(jnp.bfloat16)).reshape(factor_count * BS, group_width)
    features = jnp.concatenate([exchanged(own, t, groups) for t in range(factor_count)], axis=1)
    pre_act = jnp.dot(features, masked, preferred_element_type=jnp.float32)
    squash = jax.nn.sigmoid(pre_act)
    derivative = squash * (1.0 + pre_act * (1.0 - squash))
    grad_pre = (upstream.astype(jnp.float32) * derivative).astype(jnp.bfloat16)
    contrib = lax.dot_general(grad_pre, masked, (((1,), (1,)), ((), ())), preferred_element_type=jnp.float32)
    total = contrib[:, :BS]
    for t in range(1, factor_count):
        sent = contrib[:, t * BS : (t + 1) * BS].astype(jnp.bfloat16)
        total = total + exchanged(sent, t, groups).astype(jnp.float32)
    input_grad = lax.all_to_all(total.astype(jnp.bfloat16), "dp", 0, 1, tiled=True)
    product = lax.dot_general(features, grad_pre, (((0,), (0,)), ((), ())), preferred_element_type=jnp.float32)
    product = product.reshape(factor_count, BS, group_width) * (keep_cols.astype(jnp.float32) * (1.0 / groups))
    weight_grad = lax.all_to_all(product.astype(jnp.bfloat16), "dp", 1, 2, tiled=True)
    return (input_grad, weight_grad.astype(jnp.float32))


def body(tokens, hidden_grad, w_up, pattern):
    if lax.axis_size("dp") * BS == tokens.shape[1]:
        return body_by_group(tokens, hidden_grad, w_up, pattern)
    return body_general(tokens, hidden_grad, w_up, pattern)


def solution(mesh):
    return jax.shard_map(
        body,
        mesh=mesh,
        in_specs=(P("dp", "fly"), P("dp", "fly"), P(None, "dp", "fly"), P(None, "fly")),
        out_specs=(P("dp", "fly"), P(None, "dp", "fly")),
        check_vma=False,
    )
```

```python
import functools

import jax
import jax.numpy as jnp
from jax import lax
from jax.experimental import pallas as pl
from jax.experimental.pallas import tpu as pltpu
from jax.sharding import PartitionSpec as P

BS = 256


def partner_2(block, axis, bit):
    count = lax.axis_size(axis)
    route = []
    for low in range(count):
        high = low | 1 << bit
        if high != low and high < count:
            route += [(low, high), (high, low)]
    return lax.ppermute(block, axis, route)


def shifted(value, axis, by):
    devices = lax.axis_size(axis)
    return lax.ppermute(value, axis, [(i, (i + by) % devices) for i in range(devices)])


def flip_blocks(values, stride):
    if stride == 0:
        return values
    row_count, block_count, inner_size = values.shape
    shaped = values.reshape(row_count, block_count // (2 * stride), 2, stride, inner_size)
    return shaped[:, :, ::-1].reshape(row_count, block_count, inner_size)


def stride_of(factor):
    return 0 if factor == 0 else 2 ** (factor - 1)


def pick_rows(stacked, index, replicas):
    return lax.dynamic_index_in_dim(stacked, index % replicas, 1, keepdims=False)


def body_general(tokens, hidden_grad, w_up, pattern):
    row_count, local_width = tokens.shape
    factor_count = w_up.shape[0]
    hidden_width = hidden_grad.shape[1]
    local_blocks = local_width // BS
    group_width = hidden_width // local_blocks
    weights = lax.all_gather(w_up, "dp", axis=1, tiled=True)
    keep_cols = jnp.broadcast_to(pattern[:, :, None], (factor_count, pattern.shape[1], BS)).reshape(
        factor_count, hidden_width
    )
    masked = (weights * keep_cols.astype(jnp.bfloat16)[:, None, :]).reshape(
        factor_count, BS, local_blocks, group_width
    )
    keep_f = keep_cols.astype(jnp.float32)
    token_blocks = tokens.reshape(row_count, local_blocks, BS)
    gathered = []
    for factor in range(factor_count):
        stride = stride_of(factor)
        if stride < local_blocks:
            gathered.append(flip_blocks(token_blocks, stride))
        else:
            bit_number = (stride // local_blocks).bit_length() - 1
            partner = partner_2(tokens, "fly", bit_number)
            gathered.append(partner.reshape(row_count, local_blocks, BS))
    pre_act = jnp.zeros((row_count, local_blocks, group_width), jnp.float32)
    for factor in range(factor_count):
        pre_act = pre_act + jnp.einsum(
            "ngb,bgc->ngc", gathered[factor], masked[factor], preferred_element_type=jnp.float32
        )
    squash = jax.nn.sigmoid(pre_act)
    derivative = squash * (1.0 + pre_act * (1.0 - squash))
    grad_pre = (
        hidden_grad.reshape(row_count, local_blocks, group_width).astype(jnp.float32) * derivative
    ).astype(jnp.bfloat16)
    input_total = jnp.zeros((row_count, local_blocks, BS), jnp.float32)
    for factor in range(factor_count):
        stride = stride_of(factor)
        contrib = jnp.einsum(
            "ngc,bgc->ngb", grad_pre, masked[factor], preferred_element_type=jnp.float32
        )
        if stride < local_blocks:
            input_total = input_total + flip_blocks(contrib, stride)
        else:
            bit_number = (stride // local_blocks).bit_length() - 1
            returned = partner_2(contrib.reshape(row_count, local_width), "fly", bit_number)
            input_total = input_total + returned.reshape(row_count, local_blocks, BS)
    input_grad = input_total.reshape(row_count, local_width).astype(jnp.bfloat16)
    replicas = lax.axis_size("dp")
    place = lax.axis_index("dp")
    row_share = BS // replicas
    terms = []
    for factor in range(factor_count):
        product_term = jnp.einsum(
            "ngb,ngc->bgc", gathered[factor], grad_pre, preferred_element_type=jnp.float32
        )
        terms.append(product_term.reshape(BS, hidden_width) * keep_f[factor][None, :])
    term_stack = jnp.stack(terms).reshape(factor_count, replicas, row_share, hidden_width)

    def turn_one(step, carry):
        return shifted(carry, "dp", 1) + pick_rows(
            term_stack, place - step - 2 + 2 * replicas, replicas
        )

    summed = lax.fori_loop(
        0, replicas - 1, turn_one, pick_rows(term_stack, place - 1 + replicas, replicas)
    )
    weight_grad = summed * (1.0 / replicas)
    return (input_grad, weight_grad)


def flipped(index, by, limit):
    out, bit = 0, 1
    while bit < limit:
        differ = lax.rem(lax.div(index, jnp.int32(bit)) + lax.div(by, jnp.int32(bit)), jnp.int32(2))
        out, bit = out + differ * bit, bit * 2
    return out


def part(index, size):
    return pl.ds(pl.multiple_of(index * size, size), size)


def group_kernel(
    groups, flies, tokens, hidden_grad, w_up, pattern, sums_out, grads_out,
    feat, weights, upstream, grad_pre, masked, own_term, near_out, near_in, far_out, home_sum, product,
    token_send, token_recv, far_send, far_recv, weight_send, weight_recv, up_send, up_recv,
    pass_send, pass_recv, back_send, back_recv, other_send, other_recv, home_send, home_recv,
    grad_send, grad_recv, local_sem,
):
    me, fly = lax.axis_index("dp"), lax.axis_index("fly")
    rows = tokens.shape[0]
    factors, share = w_up.shape[0], w_up.shape[1]
    width = upstream.shape[1]
    per_group = width // BS
    half = groups // 2
    far = [t for t in range(factors) if stride_of(t) == half][0]
    near = [t for t in range(1, factors) if t != far]

    def partner(t):
        stride = stride_of(t)
        if stride < groups:
            return {"dp": flipped(me, jnp.int32(stride), groups)}
        return {"fly": flipped(fly, jnp.int32(stride // groups), flies)}

    def remote(src, dst, send, recv, device):
        return pltpu.make_async_remote_copy(
            src_ref=src, dst_ref=dst, send_sem=send, recv_sem=recv, device_id=device,
            device_id_type=pl.DeviceIdType.MESH,
        )

    def peer(k):
        return flipped(me, jnp.int32(k), groups)

    def token_copy(to, at):
        return remote(tokens.at[:, part(to, BS)], feat.at[0, part(at, rows)], token_send.at[to], token_recv.at[at], {"dp": to})

    def far_copy(to, at):
        other = flipped(to, jnp.int32(half), groups)
        return remote(tokens.at[:, part(other, BS)], feat.at[far, part(at, rows)], far_send.at[to], far_recv.at[at], {"dp": to})

    def weight_copy(to, at):
        return remote(w_up.at[:, :, part(to, width)], weights.at[:, part(at, share)], weight_send.at[to], weight_recv.at[at], {"dp": to})

    def up_copy(to, at):
        return remote(hidden_grad.at[:, part(to, width)], upstream.at[part(at, rows)], up_send.at[to], up_recv.at[at], {"dp": to})

    def pass_copy(i, s):
        t = near[i]
        return remote(feat.at[0, part(s, rows)], feat.at[t, part(s, rows)], pass_send.at[i, s], pass_recv.at[i, s], partner(t))

    def back_copy(i, s):
        return remote(near_out.at[i, part(s, rows)], near_in.at[i, part(s, rows)], back_send.at[i, s], back_recv.at[i, s], partner(near[i]))

    def other_copy(to, at):
        block = flipped(at, jnp.int32(half), groups)
        return remote(far_out.at[part(to, rows)], sums_out.at[1, :, part(block, BS)], other_send.at[to], other_recv.at[at], {"dp": to})

    def home_copy(to, at):
        return remote(home_sum.at[part(to, rows)], sums_out.at[0, :, part(at, BS)], home_send.at[to], home_recv.at[at], {"dp": to})

    def grad_copy(to, at):
        return remote(product.at[:, part(to, share)], grads_out.at[:, :, part(at, width)], grad_send.at[to], grad_recv.at[at], {"dp": to})

    barrier = pltpu.get_barrier_semaphore()
    for k in range(1, groups):
        pl.semaphore_signal(barrier, inc=1, device_id={"dp": peer(k)}, device_id_type=pl.DeviceIdType.MESH)
    across = [t for t in near if stride_of(t) >= groups]
    for t in across:
        pl.semaphore_signal(barrier, inc=1, device_id=partner(t), device_id_type=pl.DeviceIdType.MESH)
    pl.semaphore_wait(barrier, groups - 1 + len(across))

    order = list(range(groups - 1, 0, -1))
    for copy in (token_copy, far_copy, weight_copy, up_copy):
        for k in order:
            copy(peer(k), me).start()
    across_me = flipped(me, jnp.int32(half), groups)
    local = [
        pltpu.make_async_copy(tokens.at[:, part(me, BS)], feat.at[0, part(me, rows)], local_sem.at[0]),
        pltpu.make_async_copy(tokens.at[:, part(across_me, BS)], feat.at[far, part(me, rows)], local_sem.at[1]),
        pltpu.make_async_copy(w_up.at[:, :, part(me, width)], weights.at[:, part(me, share)], local_sem.at[2]),
        pltpu.make_async_copy(hidden_grad.at[:, part(me, width)], upstream.at[part(me, rows)], local_sem.at[3]),
    ]
    for copy in local:
        copy.start()

    local[0].wait()
    for i in range(len(near)):
        pass_copy(i, me).start()

    def pass_on(k, carry):
        source = flipped(me, k, groups)
        token_copy(source, source).wait_recv()
        for i in range(len(near)):
            pass_copy(i, source).start()
        return carry

    lax.fori_loop(1, groups, pass_on, 0)

    place = lax.broadcasted_iota(jnp.int32, pattern.shape, 1)
    keep = [
        jnp.sum(jnp.where(place == me * per_group + j, pattern[...], 0).astype(jnp.float32), axis=1, keepdims=True)
        for j in range(per_group)
    ]
    for copy in local[1:]:
        copy.wait()
    for k in range(1, groups):
        weight_copy(peer(k), peer(k)).wait_recv()
    for t in range(factors):
        for j in range(per_group):
            piece = weights[t, :, j * BS : (j + 1) * BS]
            masked[t * BS : (t + 1) * BS, j * BS : (j + 1) * BS] = piece * keep[j][t : t + 1].astype(jnp.bfloat16)

    def work(source):
        at = part(source, rows)
        for i in range(len(near)):
            pass_copy(i, source).wait_recv()
        features = jnp.concatenate([feat[t, at, :] for t in range(factors)], axis=1)
        pre_act = jnp.dot(features, masked[...], preferred_element_type=jnp.float32)
        squash = jax.nn.sigmoid(pre_act)
        derivative = squash * (1.0 + pre_act * (1.0 - squash))
        rounded = (upstream[at, :].astype(jnp.float32) * derivative).astype(jnp.bfloat16)
        grad_pre[at, :] = rounded
        contrib = lax.dot_general(rounded, masked[...], (((1,), (1,)), ((), ())), preferred_element_type=jnp.float32)
        own_term[at, :] = contrib[:, :BS]
        far_out[at, :] = contrib[:, far * BS : (far + 1) * BS].astype(jnp.bfloat16)
        for i, t in enumerate(near):
            near_out[i, at, :] = contrib[:, t * BS : (t + 1) * BS].astype(jnp.bfloat16)
            back_copy(i, source).start()

    work(me)
    own_far = pltpu.make_async_copy(far_out.at[part(me, rows)], sums_out.at[1, :, part(across_me, BS)], local_sem.at[1])
    own_far.start()

    def work_step(k, carry):
        source = flipped(me, k, groups)
        far_copy(source, source).wait_recv()
        up_copy(source, source).wait_recv()
        work(source)
        other_copy(source, me).start()
        return carry

    lax.fori_loop(1, groups, work_step, 0)

    for t in range(factors):
        term = lax.dot_general(feat[t], grad_pre[...], (((0,), (0,)), ((), ())), preferred_element_type=jnp.float32)
        for j in range(per_group):
            scale = keep[j][t : t + 1] * (1.0 / groups)
            product[t, :, j * BS : (j + 1) * BS] = (term[:, j * BS : (j + 1) * BS] * scale).astype(jnp.bfloat16)
    for k in order:
        grad_copy(peer(k), me).start()
    own_grad = pltpu.make_async_copy(product.at[:, part(me, share)], grads_out.at[:, :, part(me, width)], local_sem.at[2])
    own_grad.start()

    def add_up(source):
        at = part(source, rows)
        total = own_term[at, :]
        for i in range(len(near)):
            back_copy(i, source).wait_recv()
            total = total + near_in[i, at, :].astype(jnp.float32)
        home_sum[at, :] = total.astype(jnp.bfloat16)

    add_up(me)
    own_home = pltpu.make_async_copy(home_sum.at[part(me, rows)], sums_out.at[0, :, part(me, BS)], local_sem.at[0])
    own_home.start()

    def add_step(k, carry):
        source = flipped(me, k, groups)
        add_up(source)
        home_copy(source, me).start()
        return carry

    lax.fori_loop(1, groups, add_step, 0)

    def finish(k, carry):
        other = flipped(me, k, groups)
        for copy in (other_copy, home_copy, grad_copy):
            copy(other, other).wait_recv()
        for copy in (token_copy, far_copy, weight_copy, up_copy, other_copy, home_copy, grad_copy):
            copy(other, me).wait_send()
        return carry

    lax.fori_loop(1, groups, finish, 0)

    def finish_near(s, carry):
        for i in range(len(near)):
            pass_copy(i, s).wait_send()
            back_copy(i, s).wait_send()
        return carry

    lax.fori_loop(0, groups, finish_near, 0)
    own_far.wait()
    own_home.wait()
    own_grad.wait()


def body_by_group(tokens, hidden_grad, w_up, pattern):
    groups, flies = lax.axis_size("dp"), lax.axis_size("fly")
    factors, share = w_up.shape[0], w_up.shape[1]
    rows = tokens.shape[0]
    width = hidden_grad.shape[1] // groups
    every = rows * groups
    near = factors - 2
    dma = pltpu.SemaphoreType.DMA
    bf16, f32 = jnp.bfloat16, jnp.float32
    anywhere = pl.BlockSpec(memory_space=pl.ANY)
    flops = 6 * every * factors * BS * width
    sums, grads = pl.pallas_call(
        functools.partial(group_kernel, groups, flies),
        out_shape=(
            jax.ShapeDtypeStruct((2, rows, groups * BS), bf16),
            jax.ShapeDtypeStruct((factors, share, groups * width), bf16),
        ),
        in_specs=[anywhere, anywhere, anywhere, pl.BlockSpec(memory_space=pltpu.VMEM)],
        out_specs=(anywhere, anywhere),
        scratch_shapes=[
            pltpu.VMEM((factors, every, BS), bf16),
            pltpu.VMEM((factors, BS, width), bf16),
            pltpu.VMEM((every, width), bf16),
            pltpu.VMEM((every, width), bf16),
            pltpu.VMEM((factors * BS, width), bf16),
            pltpu.VMEM((every, BS), f32),
            pltpu.VMEM((near, every, BS), bf16),
            pltpu.VMEM((near, every, BS), bf16),
            pltpu.VMEM((every, BS), bf16),
            pltpu.VMEM((every, BS), bf16),
            pltpu.VMEM((factors, BS, width), bf16),
        ]
        + [dma((groups,))] * 8
        + [dma((near, groups))] * 4
        + [dma((groups,))] * 6
        + [dma((4,))],
        compiler_params=pltpu.CompilerParams(
            collective_id=0, has_side_effects=True, vmem_limit_bytes=50 * 2**20
        ),
        cost_estimate=pl.CostEstimate(flops=flops, bytes_accessed=8 * 2**20, transcendentals=every * width),
    )(tokens, hidden_grad, w_up, pattern)
    input_grad = (sums[0].astype(f32) + sums[1].astype(f32)).astype(bf16)
    return (input_grad, grads.astype(f32))


def body(tokens, hidden_grad, w_up, pattern):
    groups, flies, factors = lax.axis_size("dp"), lax.axis_size("fly"), w_up.shape[0]
    top = stride_of(factors - 1)
    if groups * BS == tokens.shape[1] and groups > 1 and groups <= top < groups * flies:
        return body_by_group(tokens, hidden_grad, w_up, pattern)
    return body_general(tokens, hidden_grad, w_up, pattern)


def solution(mesh):
    return jax.shard_map(
        body,
        mesh=mesh,
        in_specs=(P("dp", "fly"), P("dp", "fly"), P(None, "dp", "fly"), P(None, "fly")),
        out_specs=(P("dp", "fly"), P(None, "dp", "fly")),
        check_vma=False,
    )
```

```python
import functools

import jax
import jax.numpy as jnp
from jax import lax
from jax.experimental import pallas as pl
from jax.experimental.pallas import tpu as pltpu
from jax.sharding import PartitionSpec as P

BS = 256


def partner_2(block, axis, bit):
    count = lax.axis_size(axis)
    route = []
    for low in range(count):
        high = low | 1 << bit
        if high != low and high < count:
            route += [(low, high), (high, low)]
    return lax.ppermute(block, axis, route)


def shifted(value, axis, by):
    devices = lax.axis_size(axis)
    return lax.ppermute(value, axis, [(i, (i + by) % devices) for i in range(devices)])


def flip_blocks(values, stride):
    if stride == 0:
        return values
    row_count, block_count, inner_size = values.shape
    shaped = values.reshape(row_count, block_count // (2 * stride), 2, stride, inner_size)
    return shaped[:, :, ::-1].reshape(row_count, block_count, inner_size)


def stride_of(factor):
    return 0 if factor == 0 else 2 ** (factor - 1)


def pick_rows(stacked, index, replicas):
    return lax.dynamic_index_in_dim(stacked, index % replicas, 1, keepdims=False)


def body_general(tokens, hidden_grad, w_up, pattern):
    row_count, local_width = tokens.shape
    factor_count = w_up.shape[0]
    hidden_width = hidden_grad.shape[1]
    local_blocks = local_width // BS
    group_width = hidden_width // local_blocks
    weights = lax.all_gather(w_up, "dp", axis=1, tiled=True)
    keep_cols = jnp.broadcast_to(pattern[:, :, None], (factor_count, pattern.shape[1], BS)).reshape(
        factor_count, hidden_width
    )
    masked = (weights * keep_cols.astype(jnp.bfloat16)[:, None, :]).reshape(
        factor_count, BS, local_blocks, group_width
    )
    keep_f = keep_cols.astype(jnp.float32)
    token_blocks = tokens.reshape(row_count, local_blocks, BS)
    gathered = []
    for factor in range(factor_count):
        stride = stride_of(factor)
        if stride < local_blocks:
            gathered.append(flip_blocks(token_blocks, stride))
        else:
            bit_number = (stride // local_blocks).bit_length() - 1
            partner = partner_2(tokens, "fly", bit_number)
            gathered.append(partner.reshape(row_count, local_blocks, BS))
    pre_act = jnp.zeros((row_count, local_blocks, group_width), jnp.float32)
    for factor in range(factor_count):
        pre_act = pre_act + jnp.einsum(
            "ngb,bgc->ngc", gathered[factor], masked[factor], preferred_element_type=jnp.float32
        )
    squash = jax.nn.sigmoid(pre_act)
    derivative = squash * (1.0 + pre_act * (1.0 - squash))
    grad_pre = (
        hidden_grad.reshape(row_count, local_blocks, group_width).astype(jnp.float32) * derivative
    ).astype(jnp.bfloat16)
    input_total = jnp.zeros((row_count, local_blocks, BS), jnp.float32)
    for factor in range(factor_count):
        stride = stride_of(factor)
        contrib = jnp.einsum(
            "ngc,bgc->ngb", grad_pre, masked[factor], preferred_element_type=jnp.float32
        )
        if stride < local_blocks:
            input_total = input_total + flip_blocks(contrib, stride)
        else:
            bit_number = (stride // local_blocks).bit_length() - 1
            returned = partner_2(contrib.reshape(row_count, local_width), "fly", bit_number)
            input_total = input_total + returned.reshape(row_count, local_blocks, BS)
    input_grad = input_total.reshape(row_count, local_width).astype(jnp.bfloat16)
    replicas = lax.axis_size("dp")
    place = lax.axis_index("dp")
    row_share = BS // replicas
    terms = []
    for factor in range(factor_count):
        product_term = jnp.einsum(
            "ngb,ngc->bgc", gathered[factor], grad_pre, preferred_element_type=jnp.float32
        )
        terms.append(product_term.reshape(BS, hidden_width) * keep_f[factor][None, :])
    term_stack = jnp.stack(terms).reshape(factor_count, replicas, row_share, hidden_width)

    def turn_one(step, carry):
        return shifted(carry, "dp", 1) + pick_rows(
            term_stack, place - step - 2 + 2 * replicas, replicas
        )

    summed = lax.fori_loop(
        0, replicas - 1, turn_one, pick_rows(term_stack, place - 1 + replicas, replicas)
    )
    weight_grad = summed * (1.0 / replicas)
    return (input_grad, weight_grad)


def flipped(index, by, limit):
    out, bit = 0, 1
    while bit < limit:
        differ = lax.rem(lax.div(index, jnp.int32(bit)) + lax.div(by, jnp.int32(bit)), jnp.int32(2))
        out, bit = out + differ * bit, bit * 2
    return out


def part(index, size):
    return pl.ds(pl.multiple_of(index * size, size), size)


def group_kernel(
    groups, flies, tokens, hidden_grad, w_up, pattern, sums_out, grads_out,
    feat, weights, upstream, masked, own_term, near_out, near_in, far_out, home_sum, running, product,
    token_send, token_recv, far_send, far_recv, weight_send, weight_recv, up_send, up_recv,
    pass_send, pass_recv, back_send, back_recv, other_send, other_recv, home_send, home_recv,
    grad_send, grad_recv, local_sem,
):
    me, fly = lax.axis_index("dp"), lax.axis_index("fly")
    rows = tokens.shape[0]
    factors, share = w_up.shape[0], w_up.shape[1]
    width = upstream.shape[1]
    per_group = width // BS
    half = groups // 2
    far = [t for t in range(factors) if stride_of(t) == half][0]
    near = [t for t in range(1, factors) if t != far]

    def partner(t):
        stride = stride_of(t)
        if stride < groups:
            return {"dp": flipped(me, jnp.int32(stride), groups)}
        return {"fly": flipped(fly, jnp.int32(stride // groups), flies)}

    def remote(src, dst, send, recv, device):
        return pltpu.make_async_remote_copy(
            src_ref=src, dst_ref=dst, send_sem=send, recv_sem=recv, device_id=device,
            device_id_type=pl.DeviceIdType.MESH,
        )

    def peer(k):
        return flipped(me, jnp.int32(k), groups)

    def token_copy(to, at):
        return remote(tokens.at[:, part(to, BS)], feat.at[0, part(at, rows)], token_send.at[to], token_recv.at[at], {"dp": to})

    def far_copy(to, at):
        other = flipped(to, jnp.int32(half), groups)
        return remote(tokens.at[:, part(other, BS)], feat.at[far, part(at, rows)], far_send.at[to], far_recv.at[at], {"dp": to})

    def weight_copy(to, at):
        return remote(w_up.at[:, :, part(to, width)], weights.at[:, part(at, share)], weight_send.at[to], weight_recv.at[at], {"dp": to})

    def up_copy(to, at):
        return remote(hidden_grad.at[:, part(to, width)], upstream.at[part(at, rows)], up_send.at[to], up_recv.at[at], {"dp": to})

    def pass_copy(i, s):
        t = near[i]
        return remote(feat.at[0, part(s, rows)], feat.at[t, part(s, rows)], pass_send.at[i, s], pass_recv.at[i, s], partner(t))

    def back_copy(i, s):
        return remote(near_out.at[i, part(s, 2 * rows)], near_in.at[i, part(s, 2 * rows)], back_send.at[i, s], back_recv.at[i, s], partner(near[i]))

    def other_copy(to, at):
        block = flipped(at, jnp.int32(half), groups)
        return remote(far_out.at[part(to, rows)], sums_out.at[1, :, part(block, BS)], other_send.at[to], other_recv.at[at], {"dp": to})

    def home_copy(to, at):
        return remote(home_sum.at[part(to, rows)], sums_out.at[0, :, part(at, BS)], home_send.at[to], home_recv.at[at], {"dp": to})

    def grad_copy(t, to, at):
        return remote(product.at[t, part(to, share)], grads_out.at[t, :, part(at, width)], grad_send.at[t, to], grad_recv.at[t, at], {"dp": to})

    barrier = pltpu.get_barrier_semaphore()
    for k in range(1, groups):
        pl.semaphore_signal(barrier, inc=1, device_id={"dp": peer(k)}, device_id_type=pl.DeviceIdType.MESH)
    across = [t for t in near if stride_of(t) >= groups]
    for t in across:
        pl.semaphore_signal(barrier, inc=1, device_id=partner(t), device_id_type=pl.DeviceIdType.MESH)
    pl.semaphore_wait(barrier, groups - 1 + len(across))

    order = list(range(groups - 1, 0, -1))
    for copy in (token_copy, far_copy, weight_copy):
        for k in order:
            copy(peer(k), me).start()
    across_me = flipped(me, jnp.int32(half), groups)
    local = [
        pltpu.make_async_copy(tokens.at[:, part(me, BS)], feat.at[0, part(me, rows)], local_sem.at[0]),
        pltpu.make_async_copy(tokens.at[:, part(across_me, BS)], feat.at[far, part(me, rows)], local_sem.at[1]),
        pltpu.make_async_copy(w_up.at[:, :, part(me, width)], weights.at[:, part(me, share)], local_sem.at[2]),
        pltpu.make_async_copy(hidden_grad.at[:, part(me, width)], upstream.at[part(me, rows)], local_sem.at[3]),
    ]
    for copy in local:
        copy.start()

    local[0].wait()
    for i in range(len(near)):
        pass_copy(i, me).start()

    def pass_on(k, carry):
        source = flipped(me, k, groups)
        token_copy(source, source).wait_recv()
        for i in range(len(near)):
            pass_copy(i, source).start()
        return carry

    lax.fori_loop(1, groups, pass_on, 0)
    for k in order:
        weight_copy(peer(k), me).wait_send()
        up_copy(peer(k), me).start()

    place = lax.broadcasted_iota(jnp.int32, pattern.shape, 1)
    keep = [
        jnp.sum(jnp.where(place == me * per_group + j, pattern[...], 0).astype(jnp.float32), axis=1, keepdims=True)
        for j in range(per_group)
    ]
    for copy in local[1:]:
        copy.wait()
    for k in range(1, groups):
        weight_copy(peer(k), peer(k)).wait_recv()
    for t in range(factors):
        for j in range(per_group):
            piece = weights[t, :, j * BS : (j + 1) * BS]
            masked[t * BS : (t + 1) * BS, j * BS : (j + 1) * BS] = piece * keep[j][t : t + 1].astype(jnp.bfloat16)

    def sources(u):
        return [peer(2 * u), peer(2 * u + 1)]

    def pair(u):
        return lax.div(peer(2 * u), jnp.int32(2))

    def send_terms(u, rounded):
        at = part(pair(u), 2 * rows)
        contrib = lax.dot_general(rounded, masked[...], (((1,), (1,)), ((), ())), preferred_element_type=jnp.float32)
        own_term[at, :] = contrib[:, :BS]
        for i, t in enumerate(near):
            near_out[i, at, :] = contrib[:, t * BS : (t + 1) * BS].astype(jnp.bfloat16)
            back_copy(i, pair(u)).start()
        far_out[at, :] = contrib[:, far * BS : (far + 1) * BS].astype(jnp.bfloat16)
        for source in sources(u)[u == 0 :]:
            other_copy(source, me).start()

    pairs = groups // 2
    for u in range(pairs):
        at = part(pair(u), 2 * rows)
        for source in sources(u):
            for i in range(len(near)):
                pass_copy(i, source).wait_recv()
        for source in sources(u)[u == 0 :]:
            far_copy(source, source).wait_recv()
            up_copy(source, source).wait_recv()
        features = jnp.concatenate([feat[t, at, :] for t in range(factors)], axis=1)
        pre_act = jnp.dot(features, masked[...], preferred_element_type=jnp.float32)
        squash = jax.nn.sigmoid(pre_act)
        derivative = squash * (1.0 + pre_act * (1.0 - squash))
        rounded = (upstream[at, :].astype(jnp.float32) * derivative).astype(jnp.bfloat16)
        if u < pairs - 1:
            send_terms(u, rounded)
        for t in range(factors):
            term = lax.dot_general(feat[t, at, :], rounded, (((0,), (0,)), ((), ())), preferred_element_type=jnp.float32)
            if u > 0:
                term = running[t] + term
            if u < pairs - 1:
                running[t] = term
                continue
            for j in range(per_group):
                scale = keep[j][t : t + 1] * (1.0 / groups)
                product[t, :, j * BS : (j + 1) * BS] = (term[:, j * BS : (j + 1) * BS] * scale).astype(jnp.bfloat16)
            for k in order:
                grad_copy(t, peer(k), me).start()
        if u == pairs - 1:
            send_terms(u, rounded)
    own_far = pltpu.make_async_copy(far_out.at[part(me, rows)], sums_out.at[1, :, part(across_me, BS)], local_sem.at[1])
    own_far.start()
    own_grad = pltpu.make_async_copy(product.at[:, part(me, share)], grads_out.at[:, :, part(me, width)], local_sem.at[2])
    own_grad.start()

    for u in range(pairs):
        at = part(pair(u), 2 * rows)
        total = own_term[at, :]
        for i in range(len(near)):
            back_copy(i, pair(u)).wait_recv()
            total = total + near_in[i, at, :].astype(jnp.float32)
        home_sum[at, :] = total.astype(jnp.bfloat16)
        for source in sources(u)[u == 0 :]:
            home_copy(source, me).start()
    own_home = pltpu.make_async_copy(home_sum.at[part(me, rows)], sums_out.at[0, :, part(me, BS)], local_sem.at[0])
    own_home.start()

    def finish(k, carry):
        other = flipped(me, k, groups)
        for copy in (other_copy, home_copy):
            copy(other, other).wait_recv()
        for t in range(factors):
            grad_copy(t, other, other).wait_recv()
            grad_copy(t, other, me).wait_send()
        for copy in (token_copy, far_copy, up_copy, other_copy, home_copy):
            copy(other, me).wait_send()
        return carry

    lax.fori_loop(1, groups, finish, 0)

    def finish_near(s, carry):
        for i in range(len(near)):
            pass_copy(i, s).wait_send()
        return carry

    lax.fori_loop(0, groups, finish_near, 0)
    for u in range(pairs):
        for i in range(len(near)):
            back_copy(i, jnp.int32(u)).wait_send()
    own_far.wait()
    own_home.wait()
    own_grad.wait()


def body_by_group(tokens, hidden_grad, w_up, pattern):
    groups, flies = lax.axis_size("dp"), lax.axis_size("fly")
    factors, share = w_up.shape[0], w_up.shape[1]
    rows = tokens.shape[0]
    width = hidden_grad.shape[1] // groups
    every = rows * groups
    near = factors - 2
    dma = pltpu.SemaphoreType.DMA
    bf16, f32 = jnp.bfloat16, jnp.float32
    anywhere = pl.BlockSpec(memory_space=pltpu.HBM)
    flops = 6 * every * factors * BS * width
    sums, grads = pl.pallas_call(
        functools.partial(group_kernel, groups, flies),
        out_shape=(
            jax.ShapeDtypeStruct((2, rows, groups * BS), bf16),
            jax.ShapeDtypeStruct((factors, share, groups * width), bf16),
        ),
        in_specs=[anywhere, anywhere, anywhere, pl.BlockSpec(memory_space=pltpu.VMEM)],
        out_specs=(anywhere, anywhere),
        scratch_shapes=[
            pltpu.VMEM((factors, every, BS), bf16),
            pltpu.VMEM((factors, BS, width), bf16),
            pltpu.VMEM((every, width), bf16),
            pltpu.VMEM((factors * BS, width), bf16),
            pltpu.VMEM((every, BS), f32),
            pltpu.VMEM((near, every, BS), bf16),
            pltpu.VMEM((near, every, BS), bf16),
            pltpu.VMEM((every, BS), bf16),
            pltpu.VMEM((every, BS), bf16),
            pltpu.VMEM((factors, BS, width), f32),
            pltpu.VMEM((factors, BS, width), bf16),
        ]
        + [dma((groups,))] * 8
        + [dma((near, groups))] * 2
        + [dma((near, groups // 2))] * 2
        + [dma((groups,))] * 4
        + [dma((factors, groups))] * 2
        + [dma((4,))],
        compiler_params=pltpu.CompilerParams(
            collective_id=0, has_side_effects=True, vmem_limit_bytes=63 * 2**20
        ),
        cost_estimate=pl.CostEstimate(flops=flops, bytes_accessed=8 * 2**20, transcendentals=every * width),
    )(tokens, hidden_grad, w_up, pattern)
    input_grad = (sums[0].astype(f32) + sums[1].astype(f32)).astype(bf16)
    return (input_grad, grads.astype(f32))


def body(tokens, hidden_grad, w_up, pattern):
    groups, flies, factors = lax.axis_size("dp"), lax.axis_size("fly"), w_up.shape[0]
    top = stride_of(factors - 1)
    if groups * BS == tokens.shape[1] and groups > 1 and groups & (groups - 1) == 0 and groups <= top < groups * flies:
        return body_by_group(tokens, hidden_grad, w_up, pattern)
    return body_general(tokens, hidden_grad, w_up, pattern)


def solution(mesh):
    return jax.shard_map(
        body,
        mesh=mesh,
        in_specs=(P("dp", "fly"), P("dp", "fly"), P(None, "dp", "fly"), P(None, "fly")),
        out_specs=(P("dp", "fly"), P(None, "dp", "fly")),
        check_vma=False,
    )
```

```python
import functools

import jax
import jax.numpy as jnp
from jax import lax
from jax.experimental import pallas as pl
from jax.experimental.pallas import tpu as pltpu
from jax.sharding import PartitionSpec as P

BS = 256


def partner_2(block, axis, bit):
    count = lax.axis_size(axis)
    route = []
    for low in range(count):
        high = low | 1 << bit
        if high != low and high < count:
            route += [(low, high), (high, low)]
    return lax.ppermute(block, axis, route)


def shifted(value, axis, by):
    devices = lax.axis_size(axis)
    return lax.ppermute(value, axis, [(i, (i + by) % devices) for i in range(devices)])


def flip_blocks(values, stride):
    if stride == 0:
        return values
    row_count, block_count, inner_size = values.shape
    shaped = values.reshape(row_count, block_count // (2 * stride), 2, stride, inner_size)
    return shaped[:, :, ::-1].reshape(row_count, block_count, inner_size)


def stride_of(factor):
    return 0 if factor == 0 else 2 ** (factor - 1)


def pick_rows(stacked, index, replicas):
    return lax.dynamic_index_in_dim(stacked, index % replicas, 1, keepdims=False)


def body_general(tokens, hidden_grad, w_up, pattern):
    row_count, local_width = tokens.shape
    factor_count = w_up.shape[0]
    hidden_width = hidden_grad.shape[1]
    local_blocks = local_width // BS
    group_width = hidden_width // local_blocks
    weights = lax.all_gather(w_up, "dp", axis=1, tiled=True)
    keep_cols = jnp.broadcast_to(pattern[:, :, None], (factor_count, pattern.shape[1], BS)).reshape(
        factor_count, hidden_width
    )
    masked = (weights * keep_cols.astype(jnp.bfloat16)[:, None, :]).reshape(
        factor_count, BS, local_blocks, group_width
    )
    keep_f = keep_cols.astype(jnp.float32)
    token_blocks = tokens.reshape(row_count, local_blocks, BS)
    gathered = []
    for factor in range(factor_count):
        stride = stride_of(factor)
        if stride < local_blocks:
            gathered.append(flip_blocks(token_blocks, stride))
        else:
            bit_number = (stride // local_blocks).bit_length() - 1
            partner = partner_2(tokens, "fly", bit_number)
            gathered.append(partner.reshape(row_count, local_blocks, BS))
    pre_act = jnp.zeros((row_count, local_blocks, group_width), jnp.float32)
    for factor in range(factor_count):
        pre_act = pre_act + jnp.einsum(
            "ngb,bgc->ngc", gathered[factor], masked[factor], preferred_element_type=jnp.float32
        )
    squash = jax.nn.sigmoid(pre_act)
    derivative = squash * (1.0 + pre_act * (1.0 - squash))
    grad_pre = (
        hidden_grad.reshape(row_count, local_blocks, group_width).astype(jnp.float32) * derivative
    ).astype(jnp.bfloat16)
    input_total = jnp.zeros((row_count, local_blocks, BS), jnp.float32)
    for factor in range(factor_count):
        stride = stride_of(factor)
        contrib = jnp.einsum(
            "ngc,bgc->ngb", grad_pre, masked[factor], preferred_element_type=jnp.float32
        )
        if stride < local_blocks:
            input_total = input_total + flip_blocks(contrib, stride)
        else:
            bit_number = (stride // local_blocks).bit_length() - 1
            returned = partner_2(contrib.reshape(row_count, local_width), "fly", bit_number)
            input_total = input_total + returned.reshape(row_count, local_blocks, BS)
    input_grad = input_total.reshape(row_count, local_width).astype(jnp.bfloat16)
    replicas = lax.axis_size("dp")
    place = lax.axis_index("dp")
    row_share = BS // replicas
    terms = []
    for factor in range(factor_count):
        product_term = jnp.einsum(
            "ngb,ngc->bgc", gathered[factor], grad_pre, preferred_element_type=jnp.float32
        )
        terms.append(product_term.reshape(BS, hidden_width) * keep_f[factor][None, :])
    term_stack = jnp.stack(terms).reshape(factor_count, replicas, row_share, hidden_width)

    def turn_one(step, carry):
        return shifted(carry, "dp", 1) + pick_rows(
            term_stack, place - step - 2 + 2 * replicas, replicas
        )

    summed = lax.fori_loop(
        0, replicas - 1, turn_one, pick_rows(term_stack, place - 1 + replicas, replicas)
    )
    weight_grad = summed * (1.0 / replicas)
    return (input_grad, weight_grad)


def flipped(index, by, limit):
    out, bit = 0, 1
    while bit < limit:
        differ = lax.rem(lax.div(index, jnp.int32(bit)) + lax.div(by, jnp.int32(bit)), jnp.int32(2))
        out, bit = out + differ * bit, bit * 2
    return out


def part(index, size):
    return pl.ds(pl.multiple_of(index * size, size), size)


def group_kernel(
    groups, flies, tokens, hidden_grad, w_up, pattern, sums_out, grads_out,
    feat, weights, upstream, masked, own_term, near_out, near_in, far_out, home_sum, running, product,
    token_send, token_recv, far_send, far_recv, weight_send, weight_recv, up_send, up_recv,
    pass_send, pass_recv, back_send, back_recv, other_send, other_recv, home_send, home_recv,
    grad_send, grad_recv, local_sem,
):
    me, fly = lax.axis_index("dp"), lax.axis_index("fly")
    rows = tokens.shape[0]
    factors, share = w_up.shape[0], w_up.shape[1]
    width = upstream.shape[1]
    per_group = width // BS
    half = groups // 2
    far = [t for t in range(factors) if stride_of(t) == half][0]
    near = [t for t in range(1, factors) if t != far]

    def partner(t):
        stride = stride_of(t)
        if stride < groups:
            return {"dp": flipped(me, jnp.int32(stride), groups)}
        return {"fly": flipped(fly, jnp.int32(stride // groups), flies)}

    def remote(src, dst, send, recv, device):
        return pltpu.make_async_remote_copy(
            src_ref=src, dst_ref=dst, send_sem=send, recv_sem=recv, device_id=device,
            device_id_type=pl.DeviceIdType.MESH,
        )

    def peer(k):
        return flipped(me, jnp.int32(k), groups)

    def token_copy(to, at):
        return remote(tokens.at[:, part(to, BS)], feat.at[0, part(at, rows)], token_send.at[to], token_recv.at[at], {"dp": to})

    def far_copy(to, at):
        other = flipped(to, jnp.int32(half), groups)
        return remote(tokens.at[:, part(other, BS)], feat.at[far, part(at, rows)], far_send.at[to], far_recv.at[at], {"dp": to})

    def weight_copy(to, at):
        return remote(w_up.at[:, :, part(to, width)], weights.at[:, part(at, share)], weight_send.at[to], weight_recv.at[at], {"dp": to})

    def up_copy(to, at):
        return remote(hidden_grad.at[:, part(to, width)], upstream.at[part(at, rows)], up_send.at[to], up_recv.at[at], {"dp": to})

    def pass_copy(i, s):
        t = near[i]
        return remote(feat.at[0, part(s, rows)], feat.at[t, part(s, rows)], pass_send.at[i, s], pass_recv.at[i, s], partner(t))

    def back_copy(i, s):
        return remote(near_out.at[i, part(s, 2 * rows)], near_in.at[i, part(s, 2 * rows)], back_send.at[i, s], back_recv.at[i, s], partner(near[i]))

    def other_copy(to, at):
        block = flipped(at, jnp.int32(half), groups)
        return remote(far_out.at[part(to, rows)], sums_out.at[1, :, part(block, BS)], other_send.at[to], other_recv.at[at], {"dp": to})

    def home_copy(to, at):
        return remote(home_sum.at[part(to, rows)], sums_out.at[0, :, part(at, BS)], home_send.at[to], home_recv.at[at], {"dp": to})

    def grad_copy(t, to, at):
        return remote(product.at[t, part(to, share)], grads_out.at[t, :, part(at, width)], grad_send.at[t, to], grad_recv.at[t, at], {"dp": to})

    barrier = pltpu.get_barrier_semaphore()
    for k in range(1, groups):
        pl.semaphore_signal(barrier, inc=1, device_id={"dp": peer(k)}, device_id_type=pl.DeviceIdType.MESH)
    across = [t for t in near if stride_of(t) >= groups]
    for t in across:
        pl.semaphore_signal(barrier, inc=1, device_id=partner(t), device_id_type=pl.DeviceIdType.MESH)
    pl.semaphore_wait(barrier, groups - 1 + len(across))

    order = []
    for k in range(half):
        order += [groups - 1 - k] + ([k + 1] if k + 1 < half else [])
    for k in order:
        token_copy(peer(k), me).start()
        far_copy(peer(k), me).start()
    for k in order:
        weight_copy(peer(k), me).start()
    across_me = flipped(me, jnp.int32(half), groups)
    local = [
        pltpu.make_async_copy(tokens.at[:, part(me, BS)], feat.at[0, part(me, rows)], local_sem.at[0]),
        pltpu.make_async_copy(tokens.at[:, part(across_me, BS)], feat.at[far, part(me, rows)], local_sem.at[1]),
        pltpu.make_async_copy(w_up.at[:, :, part(me, width)], weights.at[:, part(me, share)], local_sem.at[2]),
        pltpu.make_async_copy(hidden_grad.at[:, part(me, width)], upstream.at[part(me, rows)], local_sem.at[3]),
    ]
    for copy in local:
        copy.start()

    local[0].wait()
    for i in range(len(near)):
        pass_copy(i, me).start()

    for k in order:
        token_copy(peer(k), peer(k)).wait_recv()
        for i in range(len(near)):
            pass_copy(i, peer(k)).start()
    for k in order:
        up_copy(peer(k), me).start()

    place = lax.broadcasted_iota(jnp.int32, pattern.shape, 1)
    keep = [
        jnp.sum(jnp.where(place == me * per_group + j, pattern[...], 0).astype(jnp.float32), axis=1, keepdims=True)
        for j in range(per_group)
    ]
    for copy in local[1:]:
        copy.wait()
    for k in range(1, groups):
        weight_copy(peer(k), peer(k)).wait_recv()
    for t in range(factors):
        for j in range(per_group):
            piece = weights[t, :, j * BS : (j + 1) * BS]
            masked[t * BS : (t + 1) * BS, j * BS : (j + 1) * BS] = piece * keep[j][t : t + 1].astype(jnp.bfloat16)

    def sources(u):
        return [peer(2 * u), peer(2 * u + 1)]

    def pair(u):
        return lax.div(peer(2 * u), jnp.int32(2))

    def send_terms(u, rounded):
        at = part(pair(u), 2 * rows)
        contrib = lax.dot_general(rounded, masked[...], (((1,), (1,)), ((), ())), preferred_element_type=jnp.float32)
        own_term[at, :] = contrib[:, :BS]
        for i, t in enumerate(near):
            near_out[i, at, :] = contrib[:, t * BS : (t + 1) * BS].astype(jnp.bfloat16)
            back_copy(i, pair(u)).start()
        far_out[at, :] = contrib[:, far * BS : (far + 1) * BS].astype(jnp.bfloat16)
        for source in sources(u)[u == 0 :]:
            other_copy(source, me).start()

    pairs = groups // 2
    for u in range(pairs):
        at = part(pair(u), 2 * rows)
        for source in sources(u):
            for i in range(len(near)):
                pass_copy(i, source).wait_recv()
        for source in sources(u)[u == 0 :]:
            far_copy(source, source).wait_recv()
            up_copy(source, source).wait_recv()
        features = jnp.concatenate([feat[t, at, :] for t in range(factors)], axis=1)
        pre_act = jnp.dot(features, masked[...], preferred_element_type=jnp.float32)
        squash = jax.nn.sigmoid(pre_act)
        derivative = squash * (1.0 + pre_act * (1.0 - squash))
        rounded = (upstream[at, :].astype(jnp.float32) * derivative).astype(jnp.bfloat16)
        if u < pairs - 1:
            send_terms(u, rounded)
        for t in range(factors):
            term = lax.dot_general(feat[t, at, :], rounded, (((0,), (0,)), ((), ())), preferred_element_type=jnp.float32)
            if u > 0:
                term = running[t] + term
            if u < pairs - 1:
                running[t] = term
                continue
            for j in range(per_group):
                scale = keep[j][t : t + 1] * (1.0 / groups)
                product[t, :, j * BS : (j + 1) * BS] = (term[:, j * BS : (j + 1) * BS] * scale).astype(jnp.bfloat16)
            for k in order:
                grad_copy(t, peer(k), me).start()
        if u == pairs - 1:
            send_terms(u, rounded)
    own_far = pltpu.make_async_copy(far_out.at[part(me, rows)], sums_out.at[1, :, part(across_me, BS)], local_sem.at[1])
    own_far.start()
    own_grad = pltpu.make_async_copy(product.at[:, part(me, share)], grads_out.at[:, :, part(me, width)], local_sem.at[2])
    own_grad.start()

    for u in range(pairs):
        at = part(pair(u), 2 * rows)
        total = own_term[at, :]
        for i in range(len(near)):
            back_copy(i, pair(u)).wait_recv()
            total = total + near_in[i, at, :].astype(jnp.float32)
        home_sum[at, :] = total.astype(jnp.bfloat16)
        for source in sources(u)[u == 0 :]:
            home_copy(source, me).start()
    own_home = pltpu.make_async_copy(home_sum.at[part(me, rows)], sums_out.at[0, :, part(me, BS)], local_sem.at[0])
    own_home.start()

    def finish(k, carry):
        other = flipped(me, k, groups)
        for copy in (other_copy, home_copy):
            copy(other, other).wait_recv()
        for t in range(factors):
            grad_copy(t, other, other).wait_recv()
            grad_copy(t, other, me).wait_send()
        for copy in (token_copy, far_copy, weight_copy, up_copy, other_copy, home_copy):
            copy(other, me).wait_send()
        return carry

    lax.fori_loop(1, groups, finish, 0)

    def finish_near(s, carry):
        for i in range(len(near)):
            pass_copy(i, s).wait_send()
        return carry

    lax.fori_loop(0, groups, finish_near, 0)
    for u in range(pairs):
        for i in range(len(near)):
            back_copy(i, jnp.int32(u)).wait_send()
    own_far.wait()
    own_home.wait()
    own_grad.wait()


def body_by_group(tokens, hidden_grad, w_up, pattern):
    groups, flies = lax.axis_size("dp"), lax.axis_size("fly")
    factors, share = w_up.shape[0], w_up.shape[1]
    rows = tokens.shape[0]
    width = hidden_grad.shape[1] // groups
    every = rows * groups
    near = factors - 2
    dma = pltpu.SemaphoreType.DMA
    bf16, f32 = jnp.bfloat16, jnp.float32
    anywhere = pl.BlockSpec(memory_space=pltpu.HBM)
    flops = 6 * every * factors * BS * width
    sums, grads = pl.pallas_call(
        functools.partial(group_kernel, groups, flies),
        out_shape=(
            jax.ShapeDtypeStruct((2, rows, groups * BS), bf16),
            jax.ShapeDtypeStruct((factors, share, groups * width), bf16),
        ),
        in_specs=[anywhere, anywhere, anywhere, pl.BlockSpec(memory_space=pltpu.VMEM)],
        out_specs=(anywhere, anywhere),
        scratch_shapes=[
            pltpu.VMEM((factors, every, BS), bf16),
            pltpu.VMEM((factors, BS, width), bf16),
            pltpu.VMEM((every, width), bf16),
            pltpu.VMEM((factors * BS, width), bf16),
            pltpu.VMEM((every, BS), f32),
            pltpu.VMEM((near, every, BS), bf16),
            pltpu.VMEM((near, every, BS), bf16),
            pltpu.VMEM((every, BS), bf16),
            pltpu.VMEM((every, BS), bf16),
            pltpu.VMEM((factors, BS, width), f32),
            pltpu.VMEM((factors, BS, width), bf16),
        ]
        + [dma((groups,))] * 8
        + [dma((near, groups))] * 2
        + [dma((near, groups // 2))] * 2
        + [dma((groups,))] * 4
        + [dma((factors, groups))] * 2
        + [dma((4,))],
        compiler_params=pltpu.CompilerParams(
            collective_id=0, has_side_effects=True, vmem_limit_bytes=63 * 2**20
        ),
        cost_estimate=pl.CostEstimate(flops=flops, bytes_accessed=8 * 2**20, transcendentals=every * width),
    )(tokens, hidden_grad, w_up, pattern)
    input_grad = (sums[0].astype(f32) + sums[1].astype(f32)).astype(bf16)
    return (input_grad, grads.astype(f32))


def body(tokens, hidden_grad, w_up, pattern):
    groups, flies, factors = lax.axis_size("dp"), lax.axis_size("fly"), w_up.shape[0]
    top = stride_of(factors - 1)
    if groups * BS == tokens.shape[1] and groups > 1 and groups & (groups - 1) == 0 and groups <= top < groups * flies:
        return body_by_group(tokens, hidden_grad, w_up, pattern)
    return body_general(tokens, hidden_grad, w_up, pattern)


def solution(mesh):
    return jax.shard_map(
        body,
        mesh=mesh,
        in_specs=(P("dp", "fly"), P("dp", "fly"), P(None, "dp", "fly"), P(None, "fly")),
        out_specs=(P("dp", "fly"), P(None, "dp", "fly")),
        check_vma=False,
    )
```

```python
import functools

import jax
import jax.numpy as jnp
from jax import lax
from jax.experimental import pallas as pl
from jax.experimental.pallas import tpu as pltpu
from jax.sharding import PartitionSpec as P

BS = 256


def partner_2(block, axis, bit):
    count = lax.axis_size(axis)
    route = []
    for low in range(count):
        high = low | 1 << bit
        if high != low and high < count:
            route += [(low, high), (high, low)]
    return lax.ppermute(block, axis, route)


def shifted(value, axis, by):
    devices = lax.axis_size(axis)
    return lax.ppermute(value, axis, [(i, (i + by) % devices) for i in range(devices)])


def flip_blocks(values, stride):
    if stride == 0:
        return values
    row_count, block_count, inner_size = values.shape
    shaped = values.reshape(row_count, block_count // (2 * stride), 2, stride, inner_size)
    return shaped[:, :, ::-1].reshape(row_count, block_count, inner_size)


def stride_of(factor):
    return 0 if factor == 0 else 2 ** (factor - 1)


def pick_rows(stacked, index, replicas):
    return lax.dynamic_index_in_dim(stacked, index % replicas, 1, keepdims=False)


def body_general(tokens, hidden_grad, w_up, pattern):
    row_count, local_width = tokens.shape
    factor_count = w_up.shape[0]
    hidden_width = hidden_grad.shape[1]
    local_blocks = local_width // BS
    group_width = hidden_width // local_blocks
    weights = lax.all_gather(w_up, "dp", axis=1, tiled=True)
    keep_cols = jnp.broadcast_to(pattern[:, :, None], (factor_count, pattern.shape[1], BS)).reshape(
        factor_count, hidden_width
    )
    masked = (weights * keep_cols.astype(jnp.bfloat16)[:, None, :]).reshape(
        factor_count, BS, local_blocks, group_width
    )
    keep_f = keep_cols.astype(jnp.float32)
    token_blocks = tokens.reshape(row_count, local_blocks, BS)
    gathered = []
    for factor in range(factor_count):
        stride = stride_of(factor)
        if stride < local_blocks:
            gathered.append(flip_blocks(token_blocks, stride))
        else:
            bit_number = (stride // local_blocks).bit_length() - 1
            partner = partner_2(tokens, "fly", bit_number)
            gathered.append(partner.reshape(row_count, local_blocks, BS))
    pre_act = jnp.zeros((row_count, local_blocks, group_width), jnp.float32)
    for factor in range(factor_count):
        pre_act = pre_act + jnp.einsum(
            "ngb,bgc->ngc", gathered[factor], masked[factor], preferred_element_type=jnp.float32
        )
    squash = jax.nn.sigmoid(pre_act)
    derivative = squash * (1.0 + pre_act * (1.0 - squash))
    grad_pre = (
        hidden_grad.reshape(row_count, local_blocks, group_width).astype(jnp.float32) * derivative
    ).astype(jnp.bfloat16)
    input_total = jnp.zeros((row_count, local_blocks, BS), jnp.float32)
    for factor in range(factor_count):
        stride = stride_of(factor)
        contrib = jnp.einsum(
            "ngc,bgc->ngb", grad_pre, masked[factor], preferred_element_type=jnp.float32
        )
        if stride < local_blocks:
            input_total = input_total + flip_blocks(contrib, stride)
        else:
            bit_number = (stride // local_blocks).bit_length() - 1
            returned = partner_2(contrib.reshape(row_count, local_width), "fly", bit_number)
            input_total = input_total + returned.reshape(row_count, local_blocks, BS)
    input_grad = input_total.reshape(row_count, local_width).astype(jnp.bfloat16)
    replicas = lax.axis_size("dp")
    place = lax.axis_index("dp")
    row_share = BS // replicas
    terms = []
    for factor in range(factor_count):
        product_term = jnp.einsum(
            "ngb,ngc->bgc", gathered[factor], grad_pre, preferred_element_type=jnp.float32
        )
        terms.append(product_term.reshape(BS, hidden_width) * keep_f[factor][None, :])
    term_stack = jnp.stack(terms).reshape(factor_count, replicas, row_share, hidden_width)

    def turn_one(step, carry):
        return shifted(carry, "dp", 1) + pick_rows(
            term_stack, place - step - 2 + 2 * replicas, replicas
        )

    summed = lax.fori_loop(
        0, replicas - 1, turn_one, pick_rows(term_stack, place - 1 + replicas, replicas)
    )
    weight_grad = summed * (1.0 / replicas)
    return (input_grad, weight_grad)


def flipped(index, by, limit):
    out, bit = 0, 1
    while bit < limit:
        differ = lax.rem(lax.div(index, jnp.int32(bit)) + lax.div(by, jnp.int32(bit)), jnp.int32(2))
        out, bit = out + differ * bit, bit * 2
    return out


def part(index, size):
    return pl.ds(pl.multiple_of(index * size, size), size)


def group_kernel(
    groups, flies, tokens, hidden_grad, w_up, pattern, sums_out, grads_out,
    feat, weights, upstream, masked, own_term, near_out, near_in, far_out, home_sum, slope, grad_pre, product,
    token_send, token_recv, far_send, far_recv, weight_send, weight_recv, up_send, up_recv,
    pass_send, pass_recv, back_send, back_recv, other_send, other_recv, home_send, home_recv,
    grad_send, grad_recv, local_sem,
):
    me, fly = lax.axis_index("dp"), lax.axis_index("fly")
    rows = tokens.shape[0]
    factors, share = w_up.shape[0], w_up.shape[1]
    width = upstream.shape[1]
    per_group = width // BS
    half = groups // 2
    far = [t for t in range(factors) if stride_of(t) == half][0]
    near = [t for t in range(1, factors) if t != far]

    def partner(t):
        stride = stride_of(t)
        if stride < groups:
            return {"dp": flipped(me, jnp.int32(stride), groups)}
        return {"fly": flipped(fly, jnp.int32(stride // groups), flies)}

    def remote(src, dst, send, recv, device):
        return pltpu.make_async_remote_copy(
            src_ref=src, dst_ref=dst, send_sem=send, recv_sem=recv, device_id=device,
            device_id_type=pl.DeviceIdType.MESH,
        )

    def peer(k):
        return flipped(me, jnp.int32(k), groups)

    def token_copy(to, at):
        return remote(tokens.at[:, part(to, BS)], feat.at[0, part(at, rows)], token_send.at[to], token_recv.at[at], {"dp": to})

    def far_copy(to, at):
        other = flipped(to, jnp.int32(half), groups)
        return remote(tokens.at[:, part(other, BS)], feat.at[far, part(at, rows)], far_send.at[to], far_recv.at[at], {"dp": to})

    def weight_copy(to, at):
        return remote(w_up.at[:, :, part(to, width)], weights.at[:, part(at, share)], weight_send.at[to], weight_recv.at[at], {"dp": to})

    def up_copy(to, at):
        return remote(hidden_grad.at[:, part(to, width)], upstream.at[part(at, rows)], up_send.at[to], up_recv.at[at], {"dp": to})

    def pass_copy(i, s):
        t = near[i]
        return remote(feat.at[0, part(s, rows)], feat.at[t, part(s, rows)], pass_send.at[i, s], pass_recv.at[i, s], partner(t))

    def back_copy(i, s):
        return remote(near_out.at[i, part(s, 2 * rows)], near_in.at[i, part(s, 2 * rows)], back_send.at[i, s], back_recv.at[i, s], partner(near[i]))

    def other_copy(to, at):
        block = flipped(at, jnp.int32(half), groups)
        return remote(far_out.at[part(to, rows)], sums_out.at[1, :, part(block, BS)], other_send.at[to], other_recv.at[at], {"dp": to})

    def home_copy(to, at):
        return remote(home_sum.at[part(to, rows)], sums_out.at[0, :, part(at, BS)], home_send.at[to], home_recv.at[at], {"dp": to})

    def grad_copy(t, to, at):
        return remote(product.at[t, part(to, share)], grads_out.at[t, :, part(at, width)], grad_send.at[t, to], grad_recv.at[t, at], {"dp": to})

    barrier = pltpu.get_barrier_semaphore()
    for k in range(1, groups):
        pl.semaphore_signal(barrier, inc=1, device_id={"dp": peer(k)}, device_id_type=pl.DeviceIdType.MESH)
    across = [t for t in near if stride_of(t) >= groups]
    for t in across:
        pl.semaphore_signal(barrier, inc=1, device_id=partner(t), device_id_type=pl.DeviceIdType.MESH)
    pl.semaphore_wait(barrier, groups - 1 + len(across))

    order = list(range(groups - 1, 0, -1))
    for copy in (token_copy, far_copy, weight_copy):
        for k in order:
            copy(peer(k), me).start()
    across_me = flipped(me, jnp.int32(half), groups)
    local = [
        pltpu.make_async_copy(tokens.at[:, part(me, BS)], feat.at[0, part(me, rows)], local_sem.at[0]),
        pltpu.make_async_copy(tokens.at[:, part(across_me, BS)], feat.at[far, part(me, rows)], local_sem.at[1]),
        pltpu.make_async_copy(w_up.at[:, :, part(me, width)], weights.at[:, part(me, share)], local_sem.at[2]),
        pltpu.make_async_copy(hidden_grad.at[:, part(me, width)], upstream.at[part(me, rows)], local_sem.at[3]),
    ]
    for copy in local:
        copy.start()

    local[0].wait()
    for i in range(len(near)):
        pass_copy(i, me).start()

    def pass_on(k, carry):
        source = flipped(me, k, groups)
        token_copy(source, source).wait_recv()
        for i in range(len(near)):
            pass_copy(i, source).start()
        return carry

    lax.fori_loop(1, groups, pass_on, 0)
    for k in order:
        weight_copy(peer(k), me).wait_send()
        up_copy(peer(k), me).start()

    place = lax.broadcasted_iota(jnp.int32, pattern.shape, 1)
    keep = [
        jnp.sum(jnp.where(place == me * per_group + j, pattern[...], 0).astype(jnp.float32), axis=1, keepdims=True)
        for j in range(per_group)
    ]
    for copy in local[1:]:
        copy.wait()
    for k in range(1, groups):
        weight_copy(peer(k), peer(k)).wait_recv()
    for t in range(factors):
        for j in range(per_group):
            piece = weights[t, :, j * BS : (j + 1) * BS]
            masked[t * BS : (t + 1) * BS, j * BS : (j + 1) * BS] = piece * keep[j][t : t + 1].astype(jnp.bfloat16)

    def sources(u):
        return [peer(2 * u), peer(2 * u + 1)]

    def pair(u):
        return lax.div(peer(2 * u), jnp.int32(2))

    def send_terms(u):
        at = part(pair(u), 2 * rows)
        contrib = lax.dot_general(grad_pre[at, :], masked[...], (((1,), (1,)), ((), ())), preferred_element_type=jnp.float32)
        own_term[at, :] = contrib[:, :BS]
        for i, t in enumerate(near):
            near_out[i, at, :] = contrib[:, t * BS : (t + 1) * BS].astype(jnp.bfloat16)
            back_copy(i, pair(u)).start()
        far_out[at, :] = contrib[:, far * BS : (far + 1) * BS].astype(jnp.bfloat16)
        for source in sources(u)[u == 0 :]:
            other_copy(source, me).start()

    pairs = groups // 2
    for u in range(pairs):
        at = part(pair(u), 2 * rows)
        for source in sources(u):
            for i in range(len(near)):
                pass_copy(i, source).wait_recv()
        for source in sources(u)[u == 0 :]:
            far_copy(source, source).wait_recv()
        features = jnp.concatenate([feat[t, at, :] for t in range(factors)], axis=1)
        pre_act = jnp.dot(features, masked[...], preferred_element_type=jnp.float32)
        squash = jax.nn.sigmoid(pre_act)
        slope[at, :] = squash * (1.0 + pre_act * (1.0 - squash))
    for u in range(pairs):
        at = part(pair(u), 2 * rows)
        for source in sources(u)[u == 0 :]:
            up_copy(source, source).wait_recv()
        grad_pre[at, :] = (upstream[at, :].astype(jnp.float32) * slope[at, :]).astype(jnp.bfloat16)
    for t in range(factors):
        term = lax.dot_general(feat[t], grad_pre[...], (((0,), (0,)), ((), ())), preferred_element_type=jnp.float32)
        for j in range(per_group):
            scale = keep[j][t : t + 1] * (1.0 / groups)
            product[t, :, j * BS : (j + 1) * BS] = (term[:, j * BS : (j + 1) * BS] * scale).astype(jnp.bfloat16)
        for k in order:
            grad_copy(t, peer(k), me).start()
    for u in range(pairs):
        send_terms(u)
    own_far = pltpu.make_async_copy(far_out.at[part(me, rows)], sums_out.at[1, :, part(across_me, BS)], local_sem.at[1])
    own_far.start()
    own_grad = pltpu.make_async_copy(product.at[:, part(me, share)], grads_out.at[:, :, part(me, width)], local_sem.at[2])
    own_grad.start()

    for u in range(pairs):
        at = part(pair(u), 2 * rows)
        total = own_term[at, :]
        for i in range(len(near)):
            back_copy(i, pair(u)).wait_recv()
            total = total + near_in[i, at, :].astype(jnp.float32)
        home_sum[at, :] = total.astype(jnp.bfloat16)
        for source in sources(u)[u == 0 :]:
            home_copy(source, me).start()
    own_home = pltpu.make_async_copy(home_sum.at[part(me, rows)], sums_out.at[0, :, part(me, BS)], local_sem.at[0])
    own_home.start()

    def finish(k, carry):
        other = flipped(me, k, groups)
        for copy in (other_copy, home_copy):
            copy(other, other).wait_recv()
        for t in range(factors):
            grad_copy(t, other, other).wait_recv()
            grad_copy(t, other, me).wait_send()
        for copy in (token_copy, far_copy, up_copy, other_copy, home_copy):
            copy(other, me).wait_send()
        return carry

    lax.fori_loop(1, groups, finish, 0)

    def finish_near(s, carry):
        for i in range(len(near)):
            pass_copy(i, s).wait_send()
        return carry

    lax.fori_loop(0, groups, finish_near, 0)
    for u in range(pairs):
        for i in range(len(near)):
            back_copy(i, jnp.int32(u)).wait_send()
    own_far.wait()
    own_home.wait()
    own_grad.wait()


def body_by_group(tokens, hidden_grad, w_up, pattern):
    groups, flies = lax.axis_size("dp"), lax.axis_size("fly")
    factors, share = w_up.shape[0], w_up.shape[1]
    rows = tokens.shape[0]
    width = hidden_grad.shape[1] // groups
    every = rows * groups
    near = factors - 2
    dma = pltpu.SemaphoreType.DMA
    bf16, f32 = jnp.bfloat16, jnp.float32
    anywhere = pl.BlockSpec(memory_space=pltpu.HBM)
    flops = 6 * every * factors * BS * width
    sums, grads = pl.pallas_call(
        functools.partial(group_kernel, groups, flies),
        out_shape=(
            jax.ShapeDtypeStruct((2, rows, groups * BS), bf16),
            jax.ShapeDtypeStruct((factors, share, groups * width), bf16),
        ),
        in_specs=[anywhere, anywhere, anywhere, pl.BlockSpec(memory_space=pltpu.VMEM)],
        out_specs=(anywhere, anywhere),
        scratch_shapes=[
            pltpu.VMEM((factors, every, BS), bf16),
            pltpu.VMEM((factors, BS, width), bf16),
            pltpu.VMEM((every, width), bf16),
            pltpu.VMEM((factors * BS, width), bf16),
            pltpu.VMEM((every, BS), f32),
            pltpu.VMEM((near, every, BS), bf16),
            pltpu.VMEM((near, every, BS), bf16),
            pltpu.VMEM((every, BS), bf16),
            pltpu.VMEM((every, BS), bf16),
            pltpu.VMEM((every, width), f32),
            pltpu.VMEM((every, width), bf16),
            pltpu.VMEM((factors, BS, width), bf16),
        ]
        + [dma((groups,))] * 8
        + [dma((near, groups))] * 2
        + [dma((near, groups // 2))] * 2
        + [dma((groups,))] * 4
        + [dma((factors, groups))] * 2
        + [dma((4,))],
        compiler_params=pltpu.CompilerParams(
            collective_id=0, has_side_effects=True, vmem_limit_bytes=63 * 2**20
        ),
        cost_estimate=pl.CostEstimate(flops=flops, bytes_accessed=8 * 2**20, transcendentals=every * width),
    )(tokens, hidden_grad, w_up, pattern)
    input_grad = (sums[0].astype(f32) + sums[1].astype(f32)).astype(bf16)
    return (input_grad, grads.astype(f32))


def body(tokens, hidden_grad, w_up, pattern):
    groups, flies, factors = lax.axis_size("dp"), lax.axis_size("fly"), w_up.shape[0]
    top = stride_of(factors - 1)
    if groups * BS == tokens.shape[1] and groups > 1 and groups & (groups - 1) == 0 and groups <= top < groups * flies:
        return body_by_group(tokens, hidden_grad, w_up, pattern)
    return body_general(tokens, hidden_grad, w_up, pattern)


def solution(mesh):
    return jax.shard_map(
        body,
        mesh=mesh,
        in_specs=(P("dp", "fly"), P("dp", "fly"), P(None, "dp", "fly"), P(None, "fly")),
        out_specs=(P("dp", "fly"), P(None, "dp", "fly")),
        check_vma=False,
    )
```

```python
import functools

import jax
import jax.numpy as jnp
from jax import lax
from jax.experimental import pallas as pl
from jax.experimental.pallas import tpu as pltpu
from jax.sharding import PartitionSpec as P

BS = 256


def partner_2(block, axis, bit):
    count = lax.axis_size(axis)
    route = []
    for low in range(count):
        high = low | 1 << bit
        if high != low and high < count:
            route += [(low, high), (high, low)]
    return lax.ppermute(block, axis, route)


def shifted(value, axis, by):
    devices = lax.axis_size(axis)
    return lax.ppermute(value, axis, [(i, (i + by) % devices) for i in range(devices)])


def flip_blocks(values, stride):
    if stride == 0:
        return values
    row_count, block_count, inner_size = values.shape
    shaped = values.reshape(row_count, block_count // (2 * stride), 2, stride, inner_size)
    return shaped[:, :, ::-1].reshape(row_count, block_count, inner_size)


def stride_of(factor):
    return 0 if factor == 0 else 2 ** (factor - 1)


def pick_rows(stacked, index, replicas):
    return lax.dynamic_index_in_dim(stacked, index % replicas, 1, keepdims=False)


def body_general(tokens, hidden_grad, w_up, pattern):
    row_count, local_width = tokens.shape
    factor_count = w_up.shape[0]
    hidden_width = hidden_grad.shape[1]
    local_blocks = local_width // BS
    group_width = hidden_width // local_blocks
    weights = lax.all_gather(w_up, "dp", axis=1, tiled=True)
    keep_cols = jnp.broadcast_to(pattern[:, :, None], (factor_count, pattern.shape[1], BS)).reshape(
        factor_count, hidden_width
    )
    masked = (weights * keep_cols.astype(jnp.bfloat16)[:, None, :]).reshape(
        factor_count, BS, local_blocks, group_width
    )
    keep_f = keep_cols.astype(jnp.float32)
    token_blocks = tokens.reshape(row_count, local_blocks, BS)
    gathered = []
    for factor in range(factor_count):
        stride = stride_of(factor)
        if stride < local_blocks:
            gathered.append(flip_blocks(token_blocks, stride))
        else:
            bit_number = (stride // local_blocks).bit_length() - 1
            partner = partner_2(tokens, "fly", bit_number)
            gathered.append(partner.reshape(row_count, local_blocks, BS))
    pre_act = jnp.zeros((row_count, local_blocks, group_width), jnp.float32)
    for factor in range(factor_count):
        pre_act = pre_act + jnp.einsum(
            "ngb,bgc->ngc", gathered[factor], masked[factor], preferred_element_type=jnp.float32
        )
    squash = jax.nn.sigmoid(pre_act)
    derivative = squash * (1.0 + pre_act * (1.0 - squash))
    grad_pre = (
        hidden_grad.reshape(row_count, local_blocks, group_width).astype(jnp.float32) * derivative
    ).astype(jnp.bfloat16)
    input_total = jnp.zeros((row_count, local_blocks, BS), jnp.float32)
    for factor in range(factor_count):
        stride = stride_of(factor)
        contrib = jnp.einsum(
            "ngc,bgc->ngb", grad_pre, masked[factor], preferred_element_type=jnp.float32
        )
        if stride < local_blocks:
            input_total = input_total + flip_blocks(contrib, stride)
        else:
            bit_number = (stride // local_blocks).bit_length() - 1
            returned = partner_2(contrib.reshape(row_count, local_width), "fly", bit_number)
            input_total = input_total + returned.reshape(row_count, local_blocks, BS)
    input_grad = input_total.reshape(row_count, local_width).astype(jnp.bfloat16)
    replicas = lax.axis_size("dp")
    place = lax.axis_index("dp")
    row_share = BS // replicas
    terms = []
    for factor in range(factor_count):
        product_term = jnp.einsum(
            "ngb,ngc->bgc", gathered[factor], grad_pre, preferred_element_type=jnp.float32
        )
        terms.append(product_term.reshape(BS, hidden_width) * keep_f[factor][None, :])
    term_stack = jnp.stack(terms).reshape(factor_count, replicas, row_share, hidden_width)

    def turn_one(step, carry):
        return shifted(carry, "dp", 1) + pick_rows(
            term_stack, place - step - 2 + 2 * replicas, replicas
        )

    summed = lax.fori_loop(
        0, replicas - 1, turn_one, pick_rows(term_stack, place - 1 + replicas, replicas)
    )
    weight_grad = summed * (1.0 / replicas)
    return (input_grad, weight_grad)


def flipped(index, by, limit):
    out, bit = 0, 1
    while bit < limit:
        differ = lax.rem(lax.div(index, jnp.int32(bit)) + lax.div(by, jnp.int32(bit)), jnp.int32(2))
        out, bit = out + differ * bit, bit * 2
    return out


def part(index, size):
    return pl.ds(pl.multiple_of(index * size, size), size)


def group_kernel(
    groups, flies, tokens, hidden_grad, w_up, pattern, sums_out, grads_out,
    feat, weights, upstream, masked, own_term, near_out, near_in, far_out, home_sum, slope, grad_pre, product,
    token_send, token_recv, far_send, far_recv, weight_send, weight_recv, up_send, up_recv,
    pass_send, pass_recv, back_send, back_recv, other_send, other_recv, home_send, home_recv,
    grad_send, grad_recv, local_sem,
):
    me, fly = lax.axis_index("dp"), lax.axis_index("fly")
    rows = tokens.shape[0]
    factors, share = w_up.shape[0], w_up.shape[1]
    width = upstream.shape[1]
    per_group = width // BS
    half = groups // 2
    far = [t for t in range(factors) if stride_of(t) == half][0]
    near = [t for t in range(1, factors) if t != far]

    def partner(t):
        stride = stride_of(t)
        if stride < groups:
            return {"dp": flipped(me, jnp.int32(stride), groups)}
        return {"fly": flipped(fly, jnp.int32(stride // groups), flies)}

    def remote(src, dst, send, recv, device):
        return pltpu.make_async_remote_copy(
            src_ref=src, dst_ref=dst, send_sem=send, recv_sem=recv, device_id=device,
            device_id_type=pl.DeviceIdType.MESH,
        )

    def peer(k):
        return flipped(me, jnp.int32(k), groups)

    def token_copy(to, at):
        return remote(tokens.at[:, part(to, BS)], feat.at[0, part(at, rows)], token_send.at[to], token_recv.at[at], {"dp": to})

    def far_copy(to, at):
        other = flipped(to, jnp.int32(half), groups)
        return remote(tokens.at[:, part(other, BS)], feat.at[far, part(at, rows)], far_send.at[to], far_recv.at[at], {"dp": to})

    def weight_copy(to, at):
        return remote(w_up.at[:, :, part(to, width)], weights.at[:, part(at, share)], weight_send.at[to], weight_recv.at[at], {"dp": to})

    def up_copy(to, at):
        return remote(hidden_grad.at[:, part(to, width)], upstream.at[part(at, rows)], up_send.at[to], up_recv.at[at], {"dp": to})

    def pass_copy(i, s):
        t = near[i]
        return remote(feat.at[0, part(s, rows)], feat.at[t, part(s, rows)], pass_send.at[i, s], pass_recv.at[i, s], partner(t))

    def back_copy(i, s):
        return remote(near_out.at[i, part(s, 2 * rows)], near_in.at[i, part(s, 2 * rows)], back_send.at[i, s], back_recv.at[i, s], partner(near[i]))

    def other_copy(to, at):
        block = flipped(at, jnp.int32(half), groups)
        return remote(far_out.at[part(to, rows)], sums_out.at[1, :, part(block, BS)], other_send.at[to], other_recv.at[at], {"dp": to})

    def home_copy(to, at):
        return remote(home_sum.at[part(to, rows)], sums_out.at[0, :, part(at, BS)], home_send.at[to], home_recv.at[at], {"dp": to})

    def grad_copy(to, at):
        return remote(product.at[:, part(to, share)], grads_out.at[:, :, part(at, width)], grad_send.at[to], grad_recv.at[at], {"dp": to})

    barrier = pltpu.get_barrier_semaphore()
    for k in range(1, groups):
        pl.semaphore_signal(barrier, inc=1, device_id={"dp": peer(k)}, device_id_type=pl.DeviceIdType.MESH)
    across = [t for t in near if stride_of(t) >= groups]
    for t in across:
        pl.semaphore_signal(barrier, inc=1, device_id=partner(t), device_id_type=pl.DeviceIdType.MESH)
    pl.semaphore_wait(barrier, groups - 1 + len(across))

    order = list(range(groups - 1, 0, -1))
    for copy in (token_copy, far_copy, weight_copy, up_copy):
        for k in order:
            copy(peer(k), me).start()
    across_me = flipped(me, jnp.int32(half), groups)
    local = [
        pltpu.make_async_copy(tokens.at[:, part(me, BS)], feat.at[0, part(me, rows)], local_sem.at[0]),
        pltpu.make_async_copy(tokens.at[:, part(across_me, BS)], feat.at[far, part(me, rows)], local_sem.at[1]),
        pltpu.make_async_copy(w_up.at[:, :, part(me, width)], weights.at[:, part(me, share)], local_sem.at[2]),
        pltpu.make_async_copy(hidden_grad.at[:, part(me, width)], upstream.at[part(me, rows)], local_sem.at[3]),
    ]
    for copy in local:
        copy.start()

    local[0].wait()
    for i in range(len(near)):
        pass_copy(i, me).start()

    def pass_on(k, carry):
        source = flipped(me, k, groups)
        token_copy(source, source).wait_recv()
        for i in range(len(near)):
            pass_copy(i, source).start()
        return carry

    lax.fori_loop(1, groups, pass_on, 0)

    place = lax.broadcasted_iota(jnp.int32, pattern.shape, 1)
    keep = [
        jnp.sum(jnp.where(place == me * per_group + j, pattern[...], 0).astype(jnp.float32), axis=1, keepdims=True)
        for j in range(per_group)
    ]
    for copy in local[1:]:
        copy.wait()
    for k in range(1, groups):
        weight_copy(peer(k), peer(k)).wait_recv()
    for t in range(factors):
        for j in range(per_group):
            piece = weights[t, :, j * BS : (j + 1) * BS]
            masked[t * BS : (t + 1) * BS, j * BS : (j + 1) * BS] = piece * keep[j][t : t + 1].astype(jnp.bfloat16)

    def sources(u):
        return [peer(2 * u), peer(2 * u + 1)]

    def pair(u):
        return lax.div(peer(2 * u), jnp.int32(2))

    def send_terms(u):
        at = part(pair(u), 2 * rows)
        contrib = lax.dot_general(grad_pre[at, :], masked[...], (((1,), (1,)), ((), ())), preferred_element_type=jnp.float32)
        own_term[at, :] = contrib[:, :BS]
        for i, t in enumerate(near):
            near_out[i, at, :] = contrib[:, t * BS : (t + 1) * BS].astype(jnp.bfloat16)
            back_copy(i, pair(u)).start()
        far_out[at, :] = contrib[:, far * BS : (far + 1) * BS].astype(jnp.bfloat16)
        for source in sources(u)[u == 0 :]:
            other_copy(source, me).start()

    pairs = groups // 2
    for u in range(pairs):
        at = part(pair(u), 2 * rows)
        for source in sources(u):
            for i in range(len(near)):
                pass_copy(i, source).wait_recv()
        for source in sources(u)[u == 0 :]:
            far_copy(source, source).wait_recv()
        features = jnp.concatenate([feat[t, at, :] for t in range(factors)], axis=1)
        pre_act = jnp.dot(features, masked[...], preferred_element_type=jnp.float32)
        squash = jax.nn.sigmoid(pre_act)
        slope[at, :] = squash * (1.0 + pre_act * (1.0 - squash))
    for u in range(pairs):
        at = part(pair(u), 2 * rows)
        for source in sources(u)[u == 0 :]:
            up_copy(source, source).wait_recv()
        grad_pre[at, :] = (upstream[at, :].astype(jnp.float32) * slope[at, :]).astype(jnp.bfloat16)
    for t in range(factors):
        term = lax.dot_general(feat[t], grad_pre[...], (((0,), (0,)), ((), ())), preferred_element_type=jnp.float32)
        for j in range(per_group):
            scale = keep[j][t : t + 1] * (1.0 / groups)
            product[t, :, j * BS : (j + 1) * BS] = (term[:, j * BS : (j + 1) * BS] * scale).astype(jnp.bfloat16)
    for k in order:
        grad_copy(peer(k), me).start()
    for u in range(pairs):
        send_terms(u)
    own_far = pltpu.make_async_copy(far_out.at[part(me, rows)], sums_out.at[1, :, part(across_me, BS)], local_sem.at[1])
    own_far.start()
    own_grad = pltpu.make_async_copy(product.at[:, part(me, share)], grads_out.at[:, :, part(me, width)], local_sem.at[2])
    own_grad.start()

    for u in range(pairs):
        at = part(pair(u), 2 * rows)
        total = own_term[at, :]
        for i in range(len(near)):
            back_copy(i, pair(u)).wait_recv()
            total = total + near_in[i, at, :].astype(jnp.float32)
        home_sum[at, :] = total.astype(jnp.bfloat16)
        for source in sources(u)[u == 0 :]:
            home_copy(source, me).start()
    own_home = pltpu.make_async_copy(home_sum.at[part(me, rows)], sums_out.at[0, :, part(me, BS)], local_sem.at[0])
    own_home.start()

    def finish(k, carry):
        other = flipped(me, k, groups)
        for copy in (other_copy, home_copy, grad_copy):
            copy(other, other).wait_recv()
        for copy in (token_copy, far_copy, weight_copy, up_copy, other_copy, home_copy, grad_copy):
            copy(other, me).wait_send()
        return carry

    lax.fori_loop(1, groups, finish, 0)

    def finish_near(s, carry):
        for i in range(len(near)):
            pass_copy(i, s).wait_send()
        return carry

    lax.fori_loop(0, groups, finish_near, 0)
    for u in range(pairs):
        for i in range(len(near)):
            back_copy(i, jnp.int32(u)).wait_send()
    own_far.wait()
    own_home.wait()
    own_grad.wait()


def body_by_group(tokens, hidden_grad, w_up, pattern):
    groups, flies = lax.axis_size("dp"), lax.axis_size("fly")
    factors, share = w_up.shape[0], w_up.shape[1]
    rows = tokens.shape[0]
    width = hidden_grad.shape[1] // groups
    every = rows * groups
    near = factors - 2
    dma = pltpu.SemaphoreType.DMA
    bf16, f32 = jnp.bfloat16, jnp.float32
    anywhere = pl.BlockSpec(memory_space=pl.ANY)
    flops = 6 * every * factors * BS * width
    sums, grads = pl.pallas_call(
        functools.partial(group_kernel, groups, flies),
        out_shape=(
            jax.ShapeDtypeStruct((2, rows, groups * BS), bf16),
            jax.ShapeDtypeStruct((factors, share, groups * width), bf16),
        ),
        in_specs=[anywhere, anywhere, anywhere, pl.BlockSpec(memory_space=pltpu.VMEM)],
        out_specs=(anywhere, anywhere),
        scratch_shapes=[
            pltpu.VMEM((factors, every, BS), bf16),
            pltpu.VMEM((factors, BS, width), bf16),
            pltpu.VMEM((every, width), bf16),
            pltpu.VMEM((factors * BS, width), bf16),
            pltpu.VMEM((every, BS), f32),
            pltpu.VMEM((near, every, BS), bf16),
            pltpu.VMEM((near, every, BS), bf16),
            pltpu.VMEM((every, BS), bf16),
            pltpu.VMEM((every, BS), bf16),
            pltpu.VMEM((every, width), f32),
            pltpu.VMEM((every, width), bf16),
            pltpu.VMEM((factors, BS, width), bf16),
        ]
        + [dma((groups,))] * 8
        + [dma((near, groups))] * 2
        + [dma((near, groups // 2))] * 2
        + [dma((groups,))] * 6
        + [dma((4,))],
        compiler_params=pltpu.CompilerParams(
            collective_id=0, has_side_effects=True, vmem_limit_bytes=50 * 2**20
        ),
        cost_estimate=pl.CostEstimate(flops=flops, bytes_accessed=8 * 2**20, transcendentals=every * width),
    )(tokens, hidden_grad, w_up, pattern)
    input_grad = (sums[0].astype(f32) + sums[1].astype(f32)).astype(bf16)
    return (input_grad, grads.astype(f32))


def body(tokens, hidden_grad, w_up, pattern):
    groups, flies, factors = lax.axis_size("dp"), lax.axis_size("fly"), w_up.shape[0]
    top = stride_of(factors - 1)
    if groups * BS == tokens.shape[1] and groups > 1 and groups & (groups - 1) == 0 and groups <= top < groups * flies:
        return body_by_group(tokens, hidden_grad, w_up, pattern)
    return body_general(tokens, hidden_grad, w_up, pattern)


def solution(mesh):
    return jax.shard_map(
        body,
        mesh=mesh,
        in_specs=(P("dp", "fly"), P("dp", "fly"), P(None, "dp", "fly"), P(None, "fly")),
        out_specs=(P("dp", "fly"), P(None, "dp", "fly")),
        check_vma=False,
    )
```
